32 devices in a mesh: tm: 8 (over z, core), lon: 2 (over y), ens: 2 (over x).
Axes of the slice: x: 2, y: 2, z: 4, core: 2. Of those that a mesh axis runs over, the one named last changes fastest.
Arguments:
- anomalies: bfloat16 [2048, 1024], P('lon', 'ens'), may hold values from -6 to 6
- localization: bfloat16 [16, 3, 128, 128], P('lon'), may hold values from -0.3125 to 0.3125
- innovations: float32 [8, 1024], P('tm', 'lon'), may hold values from -6 to 6
- obs_cell: int32 [8, 1024], P('tm', 'lon'), may hold values from 0 to 1023
- tangent_blocks: float32 [8, 8, 128, 128], P('tm'), may hold values from -1 to 2
- tangent_order: int32 [8, 8], P('tm'), may hold values from 0 to 7, each once within a row
Outputs:
- forward_states: float32 [8, 1024, 1024], P('tm', ('ens', 'lon'))
- adjoint_states: float32 [8, 1024, 1024], P('tm', ('ens', 'lon'))
The draws below stay inside these ranges and needn't reach their ends.
Inputs may be any that keep to these rules, and one draw needn't show every extreme that they name: Observation j of a step lies in sector j // 512, at that sector's cell obs_cell. `tangent_order`: each step's row names every block index once.
All inputs are finite; a program needn't handle non-finite values.
Results may differ from the reference program's by a relative error of at most 0.015.
Values may be sent and summed in bfloat16 or wider, within the bound.
A program may use at most 64 MiB of HBM per device.

```python
import math
import jax
import jax.numpy as jnp
from jax import lax

R = 1024
BLK = 128
CELLS_DEV = 1024
OBS_DEV = 512
MAP_PIECES = 8
CYCLE_INCREMENTS = 8
NCELL = 2048
NCB = 16
NOBS = 1024
N_LON = 2


def draw_tangent_blocks(key, part):
    perturbation_random_start, gradual_random_start, spike_random_start, wobble_random_start = jax.random.split(key, 4)
    identity = jnp.eye(BLK, dtype=jnp.float32)
    noise = jnp.clip(jax.random.normal(perturbation_random_start, (CYCLE_INCREMENTS, MAP_PIECES, BLK, BLK), jnp.float32), -4.0, 4.0) * (0.25 / math.sqrt(BLK))
    slow = jax.random.uniform(gradual_random_start, (MAP_PIECES,), jnp.float32) < 0.5
    slow_rate = math.log(0.3) / CYCLE_INCREMENTS - 0.03
    fast_rate = -1.0 / 40.0 - 0.03
    damping_speed = jnp.where(slow, slow_rate, fast_rate)
    wobble_magnitude = jax.random.uniform(wobble_random_start, (CYCLE_INCREMENTS, MAP_PIECES), jnp.float32, 0.7, 1.4)
    spike_magnitude = jnp.where(jax.random.uniform(spike_random_start, (CYCLE_INCREMENTS, MAP_PIECES), jnp.float32) < 3.0 / CYCLE_INCREMENTS, 0.6, 1.0)
    growth_multiplier = jnp.exp(damping_speed[None, :] * wobble_magnitude) * spike_magnitude
    return (growth_multiplier[:, :, None, None] * (identity + noise)).astype(jnp.float32)


def with_ends(entries, own_key, smallest, largest):
    shape = entries.shape
    index_at = [jax.random.randint(jax.random.fold_in(own_key, axis), (), 0, shape[axis]) for axis in range(len(shape))]
    entries = entries.at[tuple(index_at)].set(smallest)
    longest = shape.index(max(shape))
    index_at[longest] = (index_at[longest] + 1) % shape[longest]
    return entries.at[tuple(index_at)].set(largest)


def levels(rng, extent, shards, low, high):
    def one(position, shards_of):
        draws = jax.random.uniform(jax.random.fold_in(jax.random.fold_in(rng, 6), position), (shards_of,), jnp.float32, low / len(shards), high / len(shards))
        return jnp.repeat(jnp.exp(draws), extent[position] // shards_of).reshape((-1,) + (1,) * (len(extent) - position - 1))

    gain = one(*shards[0])
    for cut in shards[1:]:
        gain = gain * one(*cut)
    return gain


def normal_values(stream_key, extent, width, limit, cuts=(), kind=jnp.bfloat16):
    loudness = levels(stream_key, extent, cuts, -0.22, 0.18) if cuts else 1.0
    result = jax.random.normal(stream_key, extent, jnp.float32) * width * loudness
    return jnp.minimum(jnp.maximum(result, -limit), limit).astype(kind)


def setup_inputs(seed: int = 0) -> dict:
    seeds = jax.random.split(jax.random.key(seed), 7)
    anomalies = normal_values(seeds[0], (NCELL, R), 1.0, 6.0, ((0, 2), (1, 2)))
    localization = normal_values(seeds[1], (NCB, 3, BLK, BLK), (3 * BLK) ** -0.5, 0.3125, ((0, 2),))
    innovations = normal_values(seeds[2], (CYCLE_INCREMENTS, NOBS), 1.0, 6.0, ((0, 8), (1, 2)), jnp.float32)
    obs_cell = with_ends(jax.random.randint(seeds[3], (CYCLE_INCREMENTS, NOBS), 0, CELLS_DEV), jax.random.fold_in(seeds[3], 1), 0, CELLS_DEV - 1).astype(jnp.int32)
    tangent_blocks = draw_tangent_blocks(jax.random.fold_in(seeds[6], 71), 0)
    tangent_order = jax.vmap(lambda own: jax.random.permutation(own, MAP_PIECES))(jax.random.split(seeds[5], CYCLE_INCREMENTS)).reshape((CYCLE_INCREMENTS, MAP_PIECES)).astype(jnp.int32)
    return {"anomalies": anomalies, "localization": localization, "innovations": innovations, "obs_cell": obs_cell, "tangent_blocks": tangent_blocks, "tangent_order": tangent_order}


precise_mode = lax.Precision.HIGHEST


def apply_forward(blocks, order, state):
    row_count = state.shape[0]
    split_point = state.reshape(row_count, MAP_PIECES, BLK)
    chosen = jnp.take(split_point, order, axis=1)
    return jnp.einsum('mic,idc->mid', chosen, blocks, precision=precise_mode).reshape(row_count, R)


def apply_adjoint(blocks, order, state):
    row_count = state.shape[0]
    split_point = state.reshape(row_count, MAP_PIECES, BLK)
    moved = jnp.einsum('mic,icd->mid', split_point, blocks, precision=precise_mode)
    placed = jnp.zeros_like(moved).at[:, order, :].set(moved)
    return placed.reshape(row_count, R)


def localize(weighted, localization):
    padded = jnp.concatenate([weighted[NCELL - BLK:], weighted, weighted[:BLK]], axis=0).astype(jnp.float32)
    stacked = padded.reshape(NCB + 2, BLK, R)
    local_ops = localization.astype(jnp.float32)
    total = jnp.zeros((NCB, BLK, R), jnp.float32)
    for offset in range(3):
        total = total + jnp.einsum('bij,bjm->bim', local_ops[:, offset], stacked[offset:offset + NCB], precision=precise_mode)
    return total.reshape(NCELL, R).astype(jnp.bfloat16)


def reference(anomalies, localization, innovations, obs_cell, tangent_blocks, tangent_order):
    scale = float(NCELL) ** -0.5
    sectors = (jnp.arange(NOBS, dtype=jnp.int32) // OBS_DEV).astype(jnp.int32)
    anomaly_float = anomalies.astype(jnp.float32)

    def forcing_step(inputs):
        innov_row, cell_row = inputs
        where_cells = (sectors * CELLS_DEV + cell_row).astype(jnp.int32)
        obs_weight = jnp.zeros((NCELL,), jnp.float32).at[where_cells].add(innov_row)
        weighted = (obs_weight[:, None] * anomaly_float).astype(jnp.bfloat16)
        localized = localize(weighted, localization)
        sector_loc = localized.astype(jnp.float32).reshape(N_LON, CELLS_DEV, R)
        sector_anom = anomaly_float.reshape(N_LON, CELLS_DEV, R)
        partial_sums = (jnp.einsum('scm,scr->smr', sector_loc, sector_anom, precision=precise_mode) * scale).astype(jnp.bfloat16)
        return jnp.sum(partial_sums.astype(jnp.float32), axis=0)

    forcing = lax.map(forcing_step, (innovations, obs_cell))

    def forward_turn(state, inputs):
        blocks, order, force = inputs
        state = apply_forward(blocks, order, state) + force
        return state, state

    def adjoint_turn(state, inputs):
        blocks, order, force = inputs
        state = apply_adjoint(blocks, order, state + force)
        return state, state

    start = jnp.zeros((R, R), jnp.float32)
    forward_states = lax.scan(forward_turn, start, (tangent_blocks, tangent_order, forcing))[1]
    adjoint_states = lax.scan(adjoint_turn, start, (tangent_blocks, tangent_order, forcing), reverse=True)[1]
    return forward_states, adjoint_states
```

```python
import functools

import jax
import jax.numpy as jnp
from jax import lax
from jax.experimental import pallas as pl
from jax.experimental.pallas import tpu as pltpu
from jax.sharding import PartitionSpec as P

BLK = 128
SUBS = 4
F32 = jnp.float32
BF16 = jnp.bfloat16


def mm(a, b):
    return jnp.dot(a, b, preferred_element_type=F32)


def weight_column(innov, cells_of, first):
    ids = first + lax.broadcasted_iota(jnp.int32, (BLK, innov.shape[1]), 0)
    return jnp.sum(jnp.where(cells_of == ids, innov, 0.0), axis=1, keepdims=True)


def kernel(
    dims,
    anom,
    local,
    innov,
    obs,
    tangent,
    order,
    fwd_out,
    adj_out,
    other,
    halo,
    halo_innov,
    halo_obs,
    weighted,
    loc_t,
    part_send,
    part_recv,
    part_own,
    force,
    force_a,
    f_in,
    f_out,
    a_in,
    a_out,
    f_now,
    a_now,
    map_f,
    map_a,
    x_send,
    x_recv,
    xf_send,
    xf_recv,
    h_send,
    h_recv,
    o_send,
    o_recv,
    r_send,
    r_recv,
    f_send,
    f_recv,
    a_send,
    a_recv,
):
    n_tm, n_lon, n_ens, rows, chunk = dims
    cells, cols = anom.shape
    n_blocks = cells // BLK
    n_pieces = tangent.shape[1]
    n_chunks = rows // chunk
    group = cols // BLK
    t, l, e = lax.axis_index("tm"), lax.axis_index("lon"), lax.axis_index("ens")
    parity = lax.rem(t, 2)
    mate = t + 1 - 2 * parity
    right, left = lax.rem(l + 1, n_lon), lax.rem(l + n_lon - 1, n_lon)

    def remote(src, dst, send, recv, where):
        return pltpu.make_async_remote_copy(
            src_ref=src,
            dst_ref=dst,
            send_sem=send,
            recv_sem=recv,
            device_id=where,
            device_id_type=pl.DeviceIdType.MESH,
        )

    def at(tt=None, ll=None, ee=None):
        return (t if tt is None else tt, l if ll is None else ll, e if ee is None else ee)

    barrier = pltpu.get_barrier_semaphore()

    def greet(where):
        pl.semaphore_signal(
            barrier, inc=1, device_id=where, device_id_type=pl.DeviceIdType.MESH
        )

    for d in range(1, n_ens):
        greet(at(ee=lax.rem(e + d, n_ens)))
    for d in range(1, n_lon):
        greet(at(ll=lax.rem(l + d, n_lon)))

    @pl.when(t > 0)
    def _():
        greet(at(tt=t - 1))

    @pl.when(t < n_tm - 1)
    def _():
        greet(at(tt=t + 1))

    ends = (t > 0).astype(jnp.int32) + (t < n_tm - 1).astype(jnp.int32)
    pl.semaphore_wait(barrier, n_ens - 1 + n_lon - 1 + ends)

    half = cells // 2
    sub = half // SUBS

    def x_copy(d, s, send, recv, where, source):
        span = pl.ds(pl.multiple_of(parity * half + s * sub, sub), sub)
        return remote(source.at[span], other.at[d - 1, span], send.at[d - 1, s], recv.at[d - 1, s], where)

    edge = pl.ds(pl.multiple_of((1 - parity) * (cells - BLK), BLK), BLK)
    toward = jnp.where(parity == 0, right, left)
    halo_copy = remote(anom.at[edge], halo.at[parity], h_send.at[0], h_recv.at[0], at(ll=toward))
    halo_copy.start()
    obs_copies = []
    for side, where in ((0, right), (1, left)):
        obs_copies.append(
            remote(innov, halo_innov.at[side], o_send.at[side], o_recv.at[side], at(ll=where))
        )
        obs_copies.append(
            remote(obs, halo_obs.at[side], o_send.at[2 + side], o_recv.at[2 + side], at(ll=where))
        )
    for copy in obs_copies:
        copy.start()
    x_copies = [
        [
            x_copy(d, s, x_send, x_recv, at(ee=lax.rem(e + d, n_ens)), anom)
            for s in range(SUBS)
        ]
        for d in range(1, n_ens)
    ]
    for s in range(SUBS):
        for d in range(1, n_ens):
            x_copies[d - 1][s].start()

    innov_row, obs_row = innov[...], obs[...]

    def weigh(b, _):
        start = pl.multiple_of(b * BLK, BLK)
        column = weight_column(innov_row, obs_row, start)
        value = column * anom[pl.ds(start, BLK), :].astype(F32)
        weighted[pl.ds(pl.multiple_of(start + BLK, BLK), BLK), :] = value.astype(BF16)
        return 0

    lax.fori_loop(0, n_blocks, weigh, 0)

    def localize(b):
        start = pl.multiple_of(b * BLK, BLK)
        ops = jnp.concatenate([local[b, 0], local[b, 1], local[b, 2]], axis=1)
        value = mm(ops, weighted[pl.ds(start, 3 * BLK), :])
        loc_t[:, pl.ds(start, BLK)] = value.T.astype(BF16)

    def inner(b, _):
        localize(b)
        return 0

    lax.fori_loop(1, n_blocks - 1, inner, 0)

    halo_copy.wait_recv()
    halo_mate = remote(halo.at[parity], halo.at[parity], h_send.at[1], h_recv.at[1], at(tt=mate))
    halo_mate.start()

    def split_map(i, _):
        block = tangent[0, i]
        high = block.astype(BF16)
        low = (block - high.astype(F32)).astype(BF16)
        map_a[i, 0:BLK, :] = high
        map_a[i, BLK : 2 * BLK, :] = low
        turned = block.T
        high = turned.astype(BF16)
        map_f[i, 0:BLK, :] = high
        map_f[i, BLK : 2 * BLK, :] = (turned - high.astype(F32)).astype(BF16)
        return 0

    lax.fori_loop(0, n_pieces, split_map, 0)

    for copy in obs_copies:
        copy.wait_recv()
    remote(
        halo.at[1 - parity], halo.at[1 - parity], h_send.at[1], h_recv.at[1], at(tt=mate)
    ).wait_recv()
    for side, first, place in ((0, cells - BLK, 0), (1, 0, cells + BLK)):
        column = weight_column(halo_innov[side], halo_obs[side], first)
        weighted[place : place + BLK, :] = (column * halo[side].astype(F32)).astype(BF16)
    localize(0)
    localize(n_blocks - 1)

    scale = float(cells * n_lon) ** (-0.5)

    def r_copy(d, k, c):
        span = pl.ds(pl.multiple_of(c * chunk, chunk), chunk)
        return remote(
            part_send.at[d - 1, k, span],
            part_recv.at[d - 1, k, span],
            r_send.at[d - 1, k, c],
            r_recv.at[d - 1, k, c],
            at(ll=lax.rem(l + d, n_lon)),
        )

    def partials(k, source):
        for d in range(1, n_lon + 1):
            dest = lax.rem(l + d, n_lon)
            mine = loc_t[pl.ds(pl.multiple_of(dest * rows, rows), rows), :]
            value = (mm(mine, source[...]) * scale).astype(BF16)
            if d < n_lon:
                part_send[d - 1, k] = value
                for c in range(n_chunks):
                    r_copy(d, k, c).start()
            else:
                part_own[k] = value

    partials(0, anom)
    mate_copies = []
    for s in range(SUBS):
        for d in range(1, n_ens):
            x_copies[d - 1][s].wait_recv()
            copy = x_copy(d, s, xf_send, xf_recv, at(tt=mate), other.at[d - 1])
            copy.start()
            mate_copies.append(copy)
    for s in range(SUBS):
        for d in range(1, n_ens):
            span = pl.ds(pl.multiple_of((1 - parity) * half + s * sub, sub), sub)
            remote(
                other.at[d - 1, span],
                other.at[d - 1, span],
                xf_send.at[d - 1, s],
                xf_recv.at[d - 1, s],
                at(tt=mate),
            ).wait_recv()
    for k in range(1, n_ens):
        partials(k, other.at[k - 1])

    slots = [order[0, i] for i in range(n_pieces)]
    inverse = []
    for j in range(n_pieces):
        place = jnp.int32(0)
        for i in range(n_pieces):
            place = jnp.where(slots[i] == j, jnp.int32(i), place)
        inverse.append(place)

    @pl.when(t == 0)
    def _():
        f_in[...] = jnp.zeros_like(f_in)

    @pl.when(t == n_tm - 1)
    def _():
        a_in[...] = jnp.zeros_like(a_in)

    def f_copy(c):
        return remote(f_out.at[c], f_in.at[c], f_send.at[c], f_recv.at[c], at(tt=lax.rem(t + 1, n_tm)))

    def a_copy(c):
        return remote(
            a_out.at[c], a_in.at[c], a_send.at[c], a_recv.at[c], at(tt=lax.rem(t + n_tm - 1, n_tm))
        )

    def gather_force(c):
        span = pl.ds(pl.multiple_of(c * chunk, chunk), chunk)
        for k in range(n_ens):
            total = part_own[k, span, :].astype(F32)
            for d in range(1, n_lon):
                r_copy(d, k, c).wait_recv()
                total = total + part_recv[d - 1, k, span, :].astype(F32)
            base = lax.rem(e - k + n_ens, n_ens) * group
            for q in range(group):
                force[c, base + q] = total[:, q * BLK : (q + 1) * BLK]

    def forward_chunk(c):
        @pl.when(t > 0)
        def _():
            f_copy(c).wait_recv()

        span = pl.ds(pl.multiple_of(c * chunk, chunk), chunk)
        f_now[...] = f_in[c]
        for i in range(n_pieces):
            state = f_now[slots[i]]
            value = mm(jnp.concatenate([state, state], axis=1), map_f[i]) + force[c, i]
            f_out[c, i] = value.astype(BF16)
            fwd_out[0, span, i * BLK : (i + 1) * BLK] = value

        @pl.when(t < n_tm - 1)
        def _():
            f_copy(c).start()

    def apply_force(c):
        for j in range(n_pieces):
            value = force[c, inverse[j]]
            high = value.astype(BF16)
            low = (value - high.astype(F32)).astype(BF16)
            both = map_a[inverse[j]]
            force_a[c, j] = mm(jnp.concatenate([high, high], axis=1), both) + mm(low, both[0:BLK])

    def adjoint_chunk(c):
        @pl.when(t < n_tm - 1)
        def _():
            a_copy(c).wait_recv()

        span = pl.ds(pl.multiple_of(c * chunk, chunk), chunk)
        a_now[...] = a_in[c]
        for j in range(n_pieces):
            state = a_now[inverse[j]]
            value = mm(jnp.concatenate([state, state], axis=1), map_a[inverse[j]]) + force_a[c, j]
            a_out[c, j] = value.astype(BF16)
            adj_out[0, span, j * BLK : (j + 1) * BLK] = value

        @pl.when(t > 0)
        def _():
            a_copy(c).start()

    def turn(s, _):
        @pl.when(s < n_chunks)
        def _():
            gather_force(s)

        c_f = s - t

        @pl.when((c_f >= 0) & (c_f < n_chunks))
        def _():
            forward_chunk(c_f)

        @pl.when(s < n_chunks)
        def _():
            apply_force(s)

        c_a = s - (n_tm - 1 - t)

        @pl.when((c_a >= 0) & (c_a < n_chunks))
        def _():
            adjoint_chunk(c_a)

        return 0

    lax.fori_loop(0, n_tm - 1 + n_chunks, turn, 0)

    halo_copy.wait_send()
    halo_mate.wait_send()
    for copy in obs_copies + mate_copies:
        copy.wait_send()
    for d in range(1, n_ens):
        for s in range(SUBS):
            x_copies[d - 1][s].wait_send()
    for d in range(1, n_lon):
        for k in range(n_ens):
            for c in range(n_chunks):
                r_copy(d, k, c).wait_send()

    @pl.when(t < n_tm - 1)
    def _():
        for c in range(n_chunks):
            f_copy(c).wait_send()

    @pl.when(t > 0)
    def _():
        for c in range(n_chunks):
            a_copy(c).wait_send()


def on_device(mesh_dims, anomalies, localization, innovations, obs_cell, tangent_blocks, tangent_order):
    n_tm, n_lon, n_ens = mesh_dims
    cells, cols = anomalies.shape
    rank = cols * n_ens
    rows = cols // n_lon
    chunk = min(64, rows)
    n_chunks = rows // chunk
    pieces = tangent_blocks.shape[1]
    obs = innovations.shape[1]
    vmem = pltpu.VMEM
    dma = pltpu.SemaphoreType.DMA
    state = (n_chunks, pieces, chunk, BLK)
    parts = (max(n_lon - 1, 1), n_ens, rows, cols)
    r_sems = (max(n_lon - 1, 1), n_ens, n_chunks)
    x_sems = (max(n_ens - 1, 1), SUBS)
    in_vmem = pl.BlockSpec(memory_space=pltpu.VMEM)
    out = jax.ShapeDtypeStruct((1, rows, rank), F32)
    return pl.pallas_call(
        functools.partial(kernel, (n_tm, n_lon, n_ens, rows, chunk)),
        out_shape=(out, out),
        in_specs=[in_vmem] * 5 + [pl.BlockSpec(memory_space=pltpu.SMEM)],
        out_specs=(in_vmem, in_vmem),
        scratch_shapes=[
            vmem((max(n_ens - 1, 1), cells, cols), BF16),
            vmem((2, BLK, cols), BF16),
            vmem((2, 1, obs), F32),
            vmem((2, 1, obs), jnp.int32),
            vmem((cells + 2 * BLK, cols), BF16),
            vmem((cols, cells), BF16),
            vmem(parts, BF16),
            vmem(parts, BF16),
            vmem((n_ens, rows, cols), BF16),
            vmem(state, F32),
            vmem(state, F32),
            vmem(state, BF16),
            vmem(state, BF16),
            vmem(state, BF16),
            vmem(state, BF16),
            vmem((pieces, chunk, BLK), BF16),
            vmem((pieces, chunk, BLK), BF16),
            vmem((pieces, 2 * BLK, BLK), BF16),
            vmem((pieces, 2 * BLK, BLK), BF16),
            dma(x_sems),
            dma(x_sems),
            dma(x_sems),
            dma(x_sems),
            dma((2,)),
            dma((2,)),
            dma((4,)),
            dma((4,)),
            dma(r_sems),
            dma(r_sems),
            dma((n_chunks,)),
            dma((n_chunks,)),
            dma((n_chunks,)),
            dma((n_chunks,)),
        ],
        compiler_params=pltpu.CompilerParams(
            collective_id=0, has_side_effects=True, vmem_limit_bytes=40 * 1024 * 1024
        ),
    )(anomalies, localization, innovations, obs_cell, tangent_blocks, tangent_order)


def solution(mesh):
    placed = (
        P("lon", "ens"),
        P("lon", None, None, None),
        P("tm", "lon"),
        P("tm", "lon"),
        P("tm", None, None, None),
        P("tm", None),
    )
    mesh_dims = tuple(mesh.shape[name] for name in ("tm", "lon", "ens"))
    return jax.shard_map(
        functools.partial(on_device, mesh_dims),
        mesh=mesh,
        in_specs=placed,
        out_specs=(P("tm", ("ens", "lon"), None), P("tm", ("ens", "lon"), None)),
        check_vma=False,
    )
```

```python
import functools

import jax
import jax.numpy as jnp
from jax import lax
from jax.experimental import pallas as pl
from jax.experimental.pallas import tpu as pltpu
from jax.sharding import PartitionSpec as P

BLK = 128
SUBS = 4
F32 = jnp.float32
BF16 = jnp.bfloat16


def mm(a, b):
    return jnp.dot(a, b, preferred_element_type=F32)


def weight_column(innov, cells_of, first):
    ids = first + lax.broadcasted_iota(jnp.int32, (BLK, innov.shape[1]), 0)
    return jnp.sum(jnp.where(cells_of == ids, innov, 0.0), axis=1, keepdims=True)


def kernel(
    dims,
    anom_h,
    local_h,
    innov_h,
    obs_h,
    tangent_h,
    order_h,
    fwd_out,
    adj_out,
    anom,
    local,
    innov,
    obs,
    tangent,
    order,
    load_sem,
    other,
    halo,
    halo_innov,
    halo_obs,
    weighted,
    loc_t,
    part_send,
    part_recv,
    part_own,
    force,
    force_a,
    f_in,
    f_out,
    a_in,
    a_out,
    f_now,
    a_now,
    map_f,
    map_a,
    x_send,
    x_recv,
    xf_send,
    xf_recv,
    h_send,
    h_recv,
    o_send,
    o_recv,
    r_send,
    r_recv,
    f_send,
    f_recv,
    a_send,
    a_recv,
):
    n_tm, n_lon, n_ens, rows, chunk = dims
    loads = [
        pltpu.make_async_copy(src, dst, load_sem.at[i])
        for i, (src, dst) in enumerate(
            (
                (innov_h, innov),
                (obs_h, obs),
                (anom_h, anom),
                (local_h, local),
                (tangent_h, tangent),
                (order_h, order),
            )
        )
    ]
    for load in loads:
        load.start()
    cells, cols = anom.shape
    n_blocks = cells // BLK
    n_pieces = tangent.shape[1]
    n_chunks = rows // chunk
    group = cols // BLK
    t, l, e = lax.axis_index("tm"), lax.axis_index("lon"), lax.axis_index("ens")
    parity = lax.rem(t, 2)
    mate = t + 1 - 2 * parity
    right, left = lax.rem(l + 1, n_lon), lax.rem(l + n_lon - 1, n_lon)

    def remote(src, dst, send, recv, where):
        return pltpu.make_async_remote_copy(
            src_ref=src,
            dst_ref=dst,
            send_sem=send,
            recv_sem=recv,
            device_id=where,
            device_id_type=pl.DeviceIdType.MESH,
        )

    def at(tt=None, ll=None, ee=None):
        return (t if tt is None else tt, l if ll is None else ll, e if ee is None else ee)

    barrier = pltpu.get_barrier_semaphore()

    def greet(where):
        pl.semaphore_signal(
            barrier, inc=1, device_id=where, device_id_type=pl.DeviceIdType.MESH
        )

    for d in range(1, n_ens):
        greet(at(ee=lax.rem(e + d, n_ens)))
    for d in range(1, n_lon):
        greet(at(ll=lax.rem(l + d, n_lon)))

    @pl.when(t > 0)
    def _():
        greet(at(tt=t - 1))

    @pl.when(t < n_tm - 1)
    def _():
        greet(at(tt=t + 1))

    ends = (t > 0).astype(jnp.int32) + (t < n_tm - 1).astype(jnp.int32)
    pl.semaphore_wait(barrier, n_ens - 1 + n_lon - 1 + ends)

    half = cells // 2
    sub = half // SUBS

    def x_copy(d, s, send, recv, where, source):
        span = pl.ds(pl.multiple_of(parity * half + s * sub, sub), sub)
        return remote(source.at[span], other.at[d - 1, span], send.at[d - 1, s], recv.at[d - 1, s], where)

    edge = pl.ds(pl.multiple_of((1 - parity) * (cells - BLK), BLK), BLK)
    toward = jnp.where(parity == 0, right, left)
    halo_copy = remote(anom_h.at[edge], halo.at[parity], h_send.at[0], h_recv.at[0], at(ll=toward))
    halo_copy.start()
    obs_copies = []
    for side, where in ((0, right), (1, left)):
        obs_copies.append(
            remote(innov_h, halo_innov.at[side], o_send.at[side], o_recv.at[side], at(ll=where))
        )
        obs_copies.append(
            remote(obs_h, halo_obs.at[side], o_send.at[2 + side], o_recv.at[2 + side], at(ll=where))
        )
    for copy in obs_copies:
        copy.start()
    x_copies = [
        [
            x_copy(d, s, x_send, x_recv, at(ee=lax.rem(e + d, n_ens)), anom_h)
            for s in range(SUBS)
        ]
        for d in range(1, n_ens)
    ]
    for s in range(SUBS):
        for d in range(1, n_ens):
            x_copies[d - 1][s].start()

    for load in loads[:3]:
        load.wait()
    innov_row, obs_row = innov[...], obs[...]

    def weigh(b, _):
        start = pl.multiple_of(b * BLK, BLK)
        column = weight_column(innov_row, obs_row, start)
        value = column * anom[pl.ds(start, BLK), :].astype(F32)
        weighted[pl.ds(pl.multiple_of(start + BLK, BLK), BLK), :] = value.astype(BF16)
        return 0

    lax.fori_loop(0, n_blocks, weigh, 0)

    def localize(b):
        start = pl.multiple_of(b * BLK, BLK)
        ops = jnp.concatenate([local[b, 0], local[b, 1], local[b, 2]], axis=1)
        value = mm(ops, weighted[pl.ds(start, 3 * BLK), :])
        loc_t[:, pl.ds(start, BLK)] = value.T.astype(BF16)

    def inner(b, _):
        localize(b)
        return 0

    loads[3].wait()
    lax.fori_loop(1, n_blocks - 1, inner, 0)

    halo_copy.wait_recv()
    halo_mate = remote(halo.at[parity], halo.at[parity], h_send.at[1], h_recv.at[1], at(tt=mate))
    halo_mate.start()

    def split_map(i, _):
        block = tangent[0, i]
        high = block.astype(BF16)
        low = (block - high.astype(F32)).astype(BF16)
        map_a[i, 0:BLK, :] = high
        map_a[i, BLK : 2 * BLK, :] = low
        turned = block.T
        high = turned.astype(BF16)
        map_f[i, 0:BLK, :] = high
        map_f[i, BLK : 2 * BLK, :] = (turned - high.astype(F32)).astype(BF16)
        return 0

    loads[4].wait()
    loads[5].wait()
    lax.fori_loop(0, n_pieces, split_map, 0)

    for copy in obs_copies:
        copy.wait_recv()
    remote(
        halo.at[1 - parity], halo.at[1 - parity], h_send.at[1], h_recv.at[1], at(tt=mate)
    ).wait_recv()
    for side, first, place in ((0, cells - BLK, 0), (1, 0, cells + BLK)):
        column = weight_column(halo_innov[side], halo_obs[side], first)
        weighted[place : place + BLK, :] = (column * halo[side].astype(F32)).astype(BF16)
    localize(0)
    localize(n_blocks - 1)

    scale = float(cells * n_lon) ** (-0.5)

    def r_copy(d, k, c):
        span = pl.ds(pl.multiple_of(c * chunk, chunk), chunk)
        return remote(
            part_send.at[d - 1, k, span],
            part_recv.at[d - 1, k, span],
            r_send.at[d - 1, k, c],
            r_recv.at[d - 1, k, c],
            at(ll=lax.rem(l + d, n_lon)),
        )

    def partials(k, source):
        for d in range(1, n_lon + 1):
            dest = lax.rem(l + d, n_lon)
            mine = loc_t[pl.ds(pl.multiple_of(dest * rows, rows), rows), :]
            value = (mm(mine, source[...]) * scale).astype(BF16)
            if d < n_lon:
                part_send[d - 1, k] = value
                for c in range(n_chunks):
                    r_copy(d, k, c).start()
            else:
                part_own[k] = value

    partials(0, anom)
    mate_copies = []
    for s in range(SUBS):
        for d in range(1, n_ens):
            x_copies[d - 1][s].wait_recv()
            copy = x_copy(d, s, xf_send, xf_recv, at(tt=mate), other.at[d - 1])
            copy.start()
            mate_copies.append(copy)
    for s in range(SUBS):
        for d in range(1, n_ens):
            span = pl.ds(pl.multiple_of((1 - parity) * half + s * sub, sub), sub)
            remote(
                other.at[d - 1, span],
                other.at[d - 1, span],
                xf_send.at[d - 1, s],
                xf_recv.at[d - 1, s],
                at(tt=mate),
            ).wait_recv()
    for k in range(1, n_ens):
        partials(k, other.at[k - 1])

    slots = [order[0, i] for i in range(n_pieces)]
    inverse = []
    for j in range(n_pieces):
        place = jnp.int32(0)
        for i in range(n_pieces):
            place = jnp.where(slots[i] == j, jnp.int32(i), place)
        inverse.append(place)

    @pl.when(t == 0)
    def _():
        f_in[...] = jnp.zeros_like(f_in)

    @pl.when(t == n_tm - 1)
    def _():
        a_in[...] = jnp.zeros_like(a_in)

    def f_copy(c):
        return remote(f_out.at[c], f_in.at[c], f_send.at[c], f_recv.at[c], at(tt=lax.rem(t + 1, n_tm)))

    def a_copy(c):
        return remote(
            a_out.at[c], a_in.at[c], a_send.at[c], a_recv.at[c], at(tt=lax.rem(t + n_tm - 1, n_tm))
        )

    def gather_force(c):
        span = pl.ds(pl.multiple_of(c * chunk, chunk), chunk)
        for k in range(n_ens):
            total = part_own[k, span, :].astype(F32)
            for d in range(1, n_lon):
                r_copy(d, k, c).wait_recv()
                total = total + part_recv[d - 1, k, span, :].astype(F32)
            base = lax.rem(e - k + n_ens, n_ens) * group
            for q in range(group):
                force[c, base + q] = total[:, q * BLK : (q + 1) * BLK]

    def forward_chunk(c):
        @pl.when(t > 0)
        def _():
            f_copy(c).wait_recv()

        span = pl.ds(pl.multiple_of(c * chunk, chunk), chunk)
        f_now[...] = f_in[c]
        for i in range(n_pieces):
            state = f_now[slots[i]]
            value = mm(jnp.concatenate([state, state], axis=1), map_f[i]) + force[c, i]
            f_out[c, i] = value.astype(BF16)
            fwd_out[0, span, i * BLK : (i + 1) * BLK] = value

        @pl.when(t < n_tm - 1)
        def _():
            f_copy(c).start()

    def apply_force(c):
        for j in range(n_pieces):
            value = force[c, inverse[j]]
            high = value.astype(BF16)
            low = (value - high.astype(F32)).astype(BF16)
            both = map_a[inverse[j]]
            force_a[c, j] = mm(jnp.concatenate([high, high], axis=1), both) + mm(low, both[0:BLK])

    def adjoint_chunk(c):
        @pl.when(t < n_tm - 1)
        def _():
            a_copy(c).wait_recv()

        span = pl.ds(pl.multiple_of(c * chunk, chunk), chunk)
        a_now[...] = a_in[c]
        for j in range(n_pieces):
            state = a_now[inverse[j]]
            value = mm(jnp.concatenate([state, state], axis=1), map_a[inverse[j]]) + force_a[c, j]
            a_out[c, j] = value.astype(BF16)
            adj_out[0, span, j * BLK : (j + 1) * BLK] = value

        @pl.when(t > 0)
        def _():
            a_copy(c).start()

    def turn(s, _):
        @pl.when(s < n_chunks)
        def _():
            gather_force(s)

        c_f = s - t

        @pl.when((c_f >= 0) & (c_f < n_chunks))
        def _():
            forward_chunk(c_f)

        @pl.when(s < n_chunks)
        def _():
            apply_force(s)

        c_a = s - (n_tm - 1 - t)

        @pl.when((c_a >= 0) & (c_a < n_chunks))
        def _():
            adjoint_chunk(c_a)

        return 0

    lax.fori_loop(0, n_tm - 1 + n_chunks, turn, 0)

    halo_copy.wait_send()
    halo_mate.wait_send()
    for copy in obs_copies + mate_copies:
        copy.wait_send()
    for d in range(1, n_ens):
        for s in range(SUBS):
            x_copies[d - 1][s].wait_send()
    for d in range(1, n_lon):
        for k in range(n_ens):
            for c in range(n_chunks):
                r_copy(d, k, c).wait_send()

    @pl.when(t < n_tm - 1)
    def _():
        for c in range(n_chunks):
            f_copy(c).wait_send()

    @pl.when(t > 0)
    def _():
        for c in range(n_chunks):
            a_copy(c).wait_send()


def on_device(mesh_dims, anomalies, localization, innovations, obs_cell, tangent_blocks, tangent_order):
    n_tm, n_lon, n_ens = mesh_dims
    cells, cols = anomalies.shape
    rank = cols * n_ens
    rows = cols // n_lon
    chunk = min(64, rows)
    n_chunks = rows // chunk
    pieces = tangent_blocks.shape[1]
    obs = innovations.shape[1]
    vmem = pltpu.VMEM
    dma = pltpu.SemaphoreType.DMA
    state = (n_chunks, pieces, chunk, BLK)
    parts = (max(n_lon - 1, 1), n_ens, rows, cols)
    r_sems = (max(n_lon - 1, 1), n_ens, n_chunks)
    x_sems = (max(n_ens - 1, 1), SUBS)
    in_vmem = pl.BlockSpec(memory_space=pltpu.VMEM)
    out = jax.ShapeDtypeStruct((1, rows, rank), F32)
    return pl.pallas_call(
        functools.partial(kernel, (n_tm, n_lon, n_ens, rows, chunk)),
        out_shape=(out, out),
        in_specs=[pl.BlockSpec(memory_space=pl.ANY)] * 6,
        out_specs=(in_vmem, in_vmem),
        scratch_shapes=[
            vmem(anomalies.shape, BF16),
            vmem(localization.shape, BF16),
            vmem(innovations.shape, F32),
            vmem(obs_cell.shape, jnp.int32),
            vmem(tangent_blocks.shape, F32),
            pltpu.SMEM(tangent_order.shape, jnp.int32),
            dma((6,)),
            vmem((max(n_ens - 1, 1), cells, cols), BF16),
            vmem((2, BLK, cols), BF16),
            vmem((2, 1, obs), F32),
            vmem((2, 1, obs), jnp.int32),
            vmem((cells + 2 * BLK, cols), BF16),
            vmem((cols, cells), BF16),
            vmem(parts, BF16),
            vmem(parts, BF16),
            vmem((n_ens, rows, cols), BF16),
            vmem(state, F32),
            vmem(state, F32),
            vmem(state, BF16),
            vmem(state, BF16),
            vmem(state, BF16),
            vmem(state, BF16),
            vmem((pieces, chunk, BLK), BF16),
            vmem((pieces, chunk, BLK), BF16),
            vmem((pieces, 2 * BLK, BLK), BF16),
            vmem((pieces, 2 * BLK, BLK), BF16),
            dma(x_sems),
            dma(x_sems),
            dma(x_sems),
            dma(x_sems),
            dma((2,)),
            dma((2,)),
            dma((4,)),
            dma((4,)),
            dma(r_sems),
            dma(r_sems),
            dma((n_chunks,)),
            dma((n_chunks,)),
            dma((n_chunks,)),
            dma((n_chunks,)),
        ],
        compiler_params=pltpu.CompilerParams(
            collective_id=0, has_side_effects=True, vmem_limit_bytes=56 * 1024 * 1024
        ),
    )(anomalies, localization, innovations, obs_cell, tangent_blocks, tangent_order)


def solution(mesh):
    placed = (
        P("lon", "ens"),
        P("lon", None, None, None),
        P("tm", "lon"),
        P("tm", "lon"),
        P("tm", None, None, None),
        P("tm", None),
    )
    mesh_dims = tuple(mesh.shape[name] for name in ("tm", "lon", "ens"))
    return jax.shard_map(
        functools.partial(on_device, mesh_dims),
        mesh=mesh,
        in_specs=placed,
        out_specs=(P("tm", ("ens", "lon"), None), P("tm", ("ens", "lon"), None)),
        check_vma=False,
    )
```

```python
import functools

import jax
import jax.numpy as jnp
from jax import lax
from jax.experimental import pallas as pl
from jax.experimental.pallas import tpu as pltpu
from jax.sharding import PartitionSpec as P

BLK = 128
SUBS = 4
LAG = 4
F32 = jnp.float32
BF16 = jnp.bfloat16


def mm(a, b):
    return jnp.dot(a, b, preferred_element_type=F32)


def weight_column(innov, cells_of, first):
    ids = first + lax.broadcasted_iota(jnp.int32, (BLK, innov.shape[1]), 0)
    return jnp.sum(jnp.where(cells_of == ids, innov, 0.0), axis=1, keepdims=True)


def kernel(
    dims,
    anom_h,
    local_h,
    innov_h,
    obs_h,
    tangent_h,
    order_h,
    fwd_out,
    adj_out,
    anom,
    local,
    innov,
    obs,
    tangent,
    order,
    load_sem,
    other,
    halo,
    halo_innov,
    halo_obs,
    weighted,
    loc_t,
    part_send,
    part_recv,
    part_own,
    force,
    force_a,
    f_in,
    f_out,
    a_in,
    a_out,
    f_now,
    a_now,
    map_f,
    map_a,
    x_send,
    x_recv,
    xf_send,
    xf_recv,
    h_send,
    h_recv,
    o_send,
    o_recv,
    r_send,
    r_recv,
    f_send,
    f_recv,
    a_send,
    a_recv,
):
    n_tm, n_lon, n_ens, rows, chunk = dims
    loads = [
        pltpu.make_async_copy(src, dst, load_sem.at[i])
        for i, (src, dst) in enumerate(
            (
                (innov_h, innov),
                (obs_h, obs),
                (anom_h, anom),
                (local_h, local),
                (tangent_h, tangent),
                (order_h, order),
            )
        )
    ]
    for load in loads:
        load.start()
    cells, cols = anom.shape
    n_blocks = cells // BLK
    n_pieces = tangent.shape[1]
    n_chunks = rows // chunk
    group = cols // BLK
    t, l, e = lax.axis_index("tm"), lax.axis_index("lon"), lax.axis_index("ens")
    parity = lax.rem(t, 2)
    mate = t + 1 - 2 * parity
    right, left = lax.rem(l + 1, n_lon), lax.rem(l + n_lon - 1, n_lon)

    def remote(src, dst, send, recv, where):
        return pltpu.make_async_remote_copy(
            src_ref=src,
            dst_ref=dst,
            send_sem=send,
            recv_sem=recv,
            device_id=where,
            device_id_type=pl.DeviceIdType.MESH,
        )

    def at(tt=None, ll=None, ee=None):
        return (t if tt is None else tt, l if ll is None else ll, e if ee is None else ee)

    barrier = pltpu.get_barrier_semaphore()

    def greet(where):
        pl.semaphore_signal(
            barrier, inc=1, device_id=where, device_id_type=pl.DeviceIdType.MESH
        )

    for d in range(1, n_ens):
        greet(at(ee=lax.rem(e + d, n_ens)))
    for d in range(1, n_lon):
        greet(at(ll=lax.rem(l + d, n_lon)))

    @pl.when(t > 0)
    def _():
        greet(at(tt=t - 1))

    @pl.when(t < n_tm - 1)
    def _():
        greet(at(tt=t + 1))

    ends = (t > 0).astype(jnp.int32) + (t < n_tm - 1).astype(jnp.int32)
    pl.semaphore_wait(barrier, n_ens - 1 + n_lon - 1 + ends)

    half = cells // 2
    sub = half // SUBS

    def x_copy(d, s, send, recv, where, source):
        span = pl.ds(pl.multiple_of(parity * half + s * sub, sub), sub)
        return remote(source.at[span], other.at[d - 1, span], send.at[d - 1, s], recv.at[d - 1, s], where)

    edge = pl.ds(pl.multiple_of((1 - parity) * (cells - BLK), BLK), BLK)
    toward = jnp.where(parity == 0, right, left)
    halo_copy = remote(anom_h.at[edge], halo.at[parity], h_send.at[0], h_recv.at[0], at(ll=toward))
    halo_copy.start()
    obs_copies = []
    for side, where in ((0, right), (1, left)):
        obs_copies.append(
            remote(innov_h, halo_innov.at[side], o_send.at[side], o_recv.at[side], at(ll=where))
        )
        obs_copies.append(
            remote(obs_h, halo_obs.at[side], o_send.at[2 + side], o_recv.at[2 + side], at(ll=where))
        )
    for copy in obs_copies:
        copy.start()
    x_copies = [
        [
            x_copy(d, s, x_send, x_recv, at(ee=lax.rem(e + d, n_ens)), anom_h)
            for s in range(SUBS)
        ]
        for d in range(1, n_ens)
    ]
    for s in range(SUBS):
        for d in range(1, n_ens):
            x_copies[d - 1][s].start()

    for load in loads[:3]:
        load.wait()
    innov_row, obs_row = innov[...], obs[...]

    def weigh(b, _):
        start = pl.multiple_of(b * BLK, BLK)
        column = weight_column(innov_row, obs_row, start)
        value = column * anom[pl.ds(start, BLK), :].astype(F32)
        weighted[pl.ds(pl.multiple_of(start + BLK, BLK), BLK), :] = value.astype(BF16)
        return 0

    lax.fori_loop(0, n_blocks, weigh, 0)

    def localize(b):
        start = pl.multiple_of(b * BLK, BLK)
        ops = jnp.concatenate([local[b, 0], local[b, 1], local[b, 2]], axis=1)
        value = mm(ops, weighted[pl.ds(start, 3 * BLK), :])
        loc_t[:, pl.ds(start, BLK)] = value.T.astype(BF16)

    def inner(b, _):
        localize(b)
        return 0

    loads[3].wait()
    lax.fori_loop(1, n_blocks - 1, inner, 0)

    halo_copy.wait_recv()
    halo_mate = remote(halo.at[parity], halo.at[parity], h_send.at[1], h_recv.at[1], at(tt=mate))
    halo_mate.start()

    def split_map(i, _):
        block = tangent[0, i]
        high = block.astype(BF16)
        low = (block - high.astype(F32)).astype(BF16)
        map_a[i, 0:BLK, :] = high
        map_a[i, BLK : 2 * BLK, :] = low
        turned = block.T
        high = turned.astype(BF16)
        map_f[i, 0:BLK, :] = high
        map_f[i, BLK : 2 * BLK, :] = (turned - high.astype(F32)).astype(BF16)
        return 0

    loads[4].wait()
    loads[5].wait()
    lax.fori_loop(0, n_pieces, split_map, 0)

    for copy in obs_copies:
        copy.wait_recv()
    remote(
        halo.at[1 - parity], halo.at[1 - parity], h_send.at[1], h_recv.at[1], at(tt=mate)
    ).wait_recv()
    for side, first, place in ((0, cells - BLK, 0), (1, 0, cells + BLK)):
        column = weight_column(halo_innov[side], halo_obs[side], first)
        weighted[place : place + BLK, :] = (column * halo[side].astype(F32)).astype(BF16)
    localize(0)
    localize(n_blocks - 1)

    scale = float(cells * n_lon) ** (-0.5)

    def r_copy(d, k, c):
        span = pl.ds(pl.multiple_of(c * chunk, chunk), chunk)
        return remote(
            part_send.at[d - 1, k, span],
            part_recv.at[d - 1, k, span],
            r_send.at[d - 1, k, c],
            r_recv.at[d - 1, k, c],
            at(ll=lax.rem(l + d, n_lon)),
        )

    def partials(k, source):
        for d in range(1, n_lon + 1):
            dest = lax.rem(l + d, n_lon)
            mine = loc_t[pl.ds(pl.multiple_of(dest * rows, rows), rows), :]
            value = (mm(mine, source[...]) * scale).astype(BF16)
            if d < n_lon:
                part_send[d - 1, k] = value
                for c in range(n_chunks):
                    r_copy(d, k, c).start()
            else:
                part_own[k] = value

    partials(0, anom)
    mate_copies = []
    for s in range(SUBS):
        for d in range(1, n_ens):
            x_copies[d - 1][s].wait_recv()
            copy = x_copy(d, s, xf_send, xf_recv, at(tt=mate), other.at[d - 1])
            copy.start()
            mate_copies.append(copy)
    for s in range(SUBS):
        for d in range(1, n_ens):
            span = pl.ds(pl.multiple_of((1 - parity) * half + s * sub, sub), sub)
            remote(
                other.at[d - 1, span],
                other.at[d - 1, span],
                xf_send.at[d - 1, s],
                xf_recv.at[d - 1, s],
                at(tt=mate),
            ).wait_recv()
    for k in range(1, n_ens):
        partials(k, other.at[k - 1])

    slots = [order[0, i] for i in range(n_pieces)]
    inverse = []
    for j in range(n_pieces):
        place = jnp.int32(0)
        for i in range(n_pieces):
            place = jnp.where(slots[i] == j, jnp.int32(i), place)
        inverse.append(place)

    @pl.when(t == 0)
    def _():
        f_in[...] = jnp.zeros_like(f_in)

    @pl.when(t == n_tm - 1)
    def _():
        a_in[...] = jnp.zeros_like(a_in)

    def f_copy(c):
        return remote(f_out.at[c], f_in.at[c], f_send.at[c], f_recv.at[c], at(tt=lax.rem(t + 1, n_tm)))

    def a_copy(c):
        return remote(
            a_out.at[c], a_in.at[c], a_send.at[c], a_recv.at[c], at(tt=lax.rem(t + n_tm - 1, n_tm))
        )

    def gather_force(c):
        span = pl.ds(pl.multiple_of(c * chunk, chunk), chunk)
        for k in range(n_ens):
            total = part_own[k, span, :].astype(F32)
            for d in range(1, n_lon):
                r_copy(d, k, c).wait_recv()
                total = total + part_recv[d - 1, k, span, :].astype(F32)
            base = lax.rem(e - k + n_ens, n_ens) * group
            for q in range(group):
                force[c, base + q] = total[:, q * BLK : (q + 1) * BLK]

    def forward_chunk(c):
        @pl.when(t > 0)
        def _():
            f_copy(c).wait_recv()

        span = pl.ds(pl.multiple_of(c * chunk, chunk), chunk)
        f_now[...] = f_in[c]
        for i in range(n_pieces):
            state = f_now[slots[i]]
            value = mm(jnp.concatenate([state, state], axis=1), map_f[i]) + force[c, i]
            f_out[c, i] = value.astype(BF16)
            fwd_out[0, span, i * BLK : (i + 1) * BLK] = value

        @pl.when(t < n_tm - 1)
        def _():
            f_copy(c).start()

    def apply_force(c):
        for j in range(n_pieces):
            value = force[c, inverse[j]]
            high = value.astype(BF16)
            low = (value - high.astype(F32)).astype(BF16)
            both = map_a[inverse[j]]
            force_a[c, j] = mm(jnp.concatenate([high, high], axis=1), both) + mm(low, both[0:BLK])

    def adjoint_chunk(c):
        @pl.when(t < n_tm - 1)
        def _():
            a_copy(c).wait_recv()

        span = pl.ds(pl.multiple_of(c * chunk, chunk), chunk)
        a_now[...] = a_in[c]
        for j in range(n_pieces):
            state = a_now[inverse[j]]
            value = mm(jnp.concatenate([state, state], axis=1), map_a[inverse[j]]) + force_a[c, j]
            a_out[c, j] = value.astype(BF16)
            adj_out[0, span, j * BLK : (j + 1) * BLK] = value

        @pl.when(t > 0)
        def _():
            a_copy(c).start()

    def turn(s, _):
        @pl.when(s < n_chunks)
        def _():
            gather_force(s)

        c_f = s - LAG * t

        @pl.when((c_f >= 0) & (c_f < n_chunks))
        def _():
            forward_chunk(c_f)

        @pl.when(s < n_chunks)
        def _():
            apply_force(s)

        c_a = s - LAG * (n_tm - 1 - t)

        @pl.when((c_a >= 0) & (c_a < n_chunks))
        def _():
            adjoint_chunk(c_a)

        return 0

    lax.fori_loop(0, LAG * (n_tm - 1) + n_chunks, turn, 0)

    halo_copy.wait_send()
    halo_mate.wait_send()
    for copy in obs_copies + mate_copies:
        copy.wait_send()
    for d in range(1, n_ens):
        for s in range(SUBS):
            x_copies[d - 1][s].wait_send()
    for d in range(1, n_lon):
        for k in range(n_ens):
            for c in range(n_chunks):
                r_copy(d, k, c).wait_send()

    @pl.when(t < n_tm - 1)
    def _():
        for c in range(n_chunks):
            f_copy(c).wait_send()

    @pl.when(t > 0)
    def _():
        for c in range(n_chunks):
            a_copy(c).wait_send()


def on_device(mesh_dims, anomalies, localization, innovations, obs_cell, tangent_blocks, tangent_order):
    n_tm, n_lon, n_ens = mesh_dims
    cells, cols = anomalies.shape
    rank = cols * n_ens
    rows = cols // n_lon
    chunk = min(32, rows)
    n_chunks = rows // chunk
    pieces = tangent_blocks.shape[1]
    obs = innovations.shape[1]
    vmem = pltpu.VMEM
    dma = pltpu.SemaphoreType.DMA
    state = (n_chunks, pieces, chunk, BLK)
    parts = (max(n_lon - 1, 1), n_ens, rows, cols)
    r_sems = (max(n_lon - 1, 1), n_ens, n_chunks)
    x_sems = (max(n_ens - 1, 1), SUBS)
    in_vmem = pl.BlockSpec(memory_space=pltpu.VMEM)
    out = jax.ShapeDtypeStruct((1, rows, rank), F32)
    return pl.pallas_call(
        functools.partial(kernel, (n_tm, n_lon, n_ens, rows, chunk)),
        out_shape=(out, out),
        in_specs=[pl.BlockSpec(memory_space=pl.ANY)] * 6,
        out_specs=(in_vmem, in_vmem),
        scratch_shapes=[
            vmem(anomalies.shape, BF16),
            vmem(localization.shape, BF16),
            vmem(innovations.shape, F32),
            vmem(obs_cell.shape, jnp.int32),
            vmem(tangent_blocks.shape, F32),
            pltpu.SMEM(tangent_order.shape, jnp.int32),
            dma((6,)),
            vmem((max(n_ens - 1, 1), cells, cols), BF16),
            vmem((2, BLK, cols), BF16),
            vmem((2, 1, obs), F32),
            vmem((2, 1, obs), jnp.int32),
            vmem((cells + 2 * BLK, cols), BF16),
            vmem((cols, cells), BF16),
            vmem(parts, BF16),
            vmem(parts, BF16),
            vmem((n_ens, rows, cols), BF16),
            vmem(state, F32),
            vmem(state, F32),
            vmem(state, BF16),
            vmem(state, BF16),
            vmem(state, BF16),
            vmem(state, BF16),
            vmem((pieces, chunk, BLK), BF16),
            vmem((pieces, chunk, BLK), BF16),
            vmem((pieces, 2 * BLK, BLK), BF16),
            vmem((pieces, 2 * BLK, BLK), BF16),
            dma(x_sems),
            dma(x_sems),
            dma(x_sems),
            dma(x_sems),
            dma((2,)),
            dma((2,)),
            dma((4,)),
            dma((4,)),
            dma(r_sems),
            dma(r_sems),
            dma((n_chunks,)),
            dma((n_chunks,)),
            dma((n_chunks,)),
            dma((n_chunks,)),
        ],
        compiler_params=pltpu.CompilerParams(
            collective_id=0, has_side_effects=True, vmem_limit_bytes=56 * 1024 * 1024
        ),
    )(anomalies, localization, innovations, obs_cell, tangent_blocks, tangent_order)


def solution(mesh):
    placed = (
        P("lon", "ens"),
        P("lon", None, None, None),
        P("tm", "lon"),
        P("tm", "lon"),
        P("tm", None, None, None),
        P("tm", None),
    )
    mesh_dims = tuple(mesh.shape[name] for name in ("tm", "lon", "ens"))
    return jax.shard_map(
        functools.partial(on_device, mesh_dims),
        mesh=mesh,
        in_specs=placed,
        out_specs=(P("tm", ("ens", "lon"), None), P("tm", ("ens", "lon"), None)),
        check_vma=False,
    )
```

```python
import functools

import jax
import jax.numpy as jnp
from jax import lax
from jax.experimental import pallas as pl
from jax.experimental.pallas import tpu as pltpu
from jax.sharding import PartitionSpec as P

BLK = 128
SUBS = 4
LAG = 4
STORES = 4
F32 = jnp.float32
BF16 = jnp.bfloat16


def mm(a, b):
    return jnp.dot(a, b, preferred_element_type=F32)


def weight_column(innov, cells_of, first):
    ids = first + lax.broadcasted_iota(jnp.int32, (BLK, innov.shape[1]), 0)
    return jnp.sum(jnp.where(cells_of == ids, innov, 0.0), axis=1, keepdims=True)


def kernel(
    dims,
    anom_h,
    local_h,
    innov_h,
    obs_h,
    tangent_h,
    order_h,
    fwd_out,
    adj_out,
    anom,
    local,
    innov,
    obs,
    tangent,
    order,
    load_sem,
    other,
    halo,
    halo_innov,
    halo_obs,
    weighted,
    loc_t,
    part_send,
    part_recv,
    part_own,
    force,
    force_a,
    f_in,
    f_out,
    a_in,
    a_out,
    f_now,
    a_now,
    map_f,
    map_a,
    x_send,
    x_recv,
    xf_send,
    xf_recv,
    h_send,
    h_recv,
    o_send,
    o_recv,
    r_send,
    r_recv,
    f_send,
    f_recv,
    a_send,
    a_recv,
):
    n_tm, n_lon, n_ens, rows, chunk = dims
    loads = [
        pltpu.make_async_copy(src, dst, load_sem.at[i])
        for i, (src, dst) in enumerate(
            (
                (innov_h, innov),
                (obs_h, obs),
                (anom_h, anom),
                (local_h, local),
                (tangent_h, tangent),
                (order_h, order),
            )
        )
    ]
    for load in loads:
        load.start()
    cells, cols = anom.shape
    n_blocks = cells // BLK
    n_pieces = tangent.shape[1]
    n_chunks = rows // chunk
    group = cols // BLK
    t, l, e = lax.axis_index("tm"), lax.axis_index("lon"), lax.axis_index("ens")
    parity = lax.rem(t, 2)
    mate = t + 1 - 2 * parity
    right, left = lax.rem(l + 1, n_lon), lax.rem(l + n_lon - 1, n_lon)

    def remote(src, dst, send, recv, where):
        return pltpu.make_async_remote_copy(
            src_ref=src,
            dst_ref=dst,
            send_sem=send,
            recv_sem=recv,
            device_id=where,
            device_id_type=pl.DeviceIdType.MESH,
        )

    def at(tt=None, ll=None, ee=None):
        return (t if tt is None else tt, l if ll is None else ll, e if ee is None else ee)

    barrier = pltpu.get_barrier_semaphore()

    def greet(where):
        pl.semaphore_signal(
            barrier, inc=1, device_id=where, device_id_type=pl.DeviceIdType.MESH
        )

    for d in range(1, n_ens):
        greet(at(ee=lax.rem(e + d, n_ens)))
    for d in range(1, n_lon):
        greet(at(ll=lax.rem(l + d, n_lon)))

    @pl.when(t > 0)
    def _():
        greet(at(tt=t - 1))

    @pl.when(t < n_tm - 1)
    def _():
        greet(at(tt=t + 1))

    ends = (t > 0).astype(jnp.int32) + (t < n_tm - 1).astype(jnp.int32)
    pl.semaphore_wait(barrier, n_ens - 1 + n_lon - 1 + ends)

    half = cells // 2
    sub = half // SUBS

    def x_copy(d, s, send, recv, where, source):
        span = pl.ds(pl.multiple_of(parity * half + s * sub, sub), sub)
        return remote(source.at[span], other.at[d - 1, span], send.at[d - 1, s], recv.at[d - 1, s], where)

    edge = pl.ds(pl.multiple_of((1 - parity) * (cells - BLK), BLK), BLK)
    toward = jnp.where(parity == 0, right, left)
    halo_copy = remote(anom_h.at[edge], halo.at[parity], h_send.at[0], h_recv.at[0], at(ll=toward))
    halo_copy.start()
    obs_copies = []
    for side, where in ((0, right), (1, left)):
        obs_copies.append(
            remote(innov_h, halo_innov.at[side], o_send.at[side], o_recv.at[side], at(ll=where))
        )
        obs_copies.append(
            remote(obs_h, halo_obs.at[side], o_send.at[2 + side], o_recv.at[2 + side], at(ll=where))
        )
    for copy in obs_copies:
        copy.start()
    x_copies = [
        [
            x_copy(d, s, x_send, x_recv, at(ee=lax.rem(e + d, n_ens)), anom_h)
            for s in range(SUBS)
        ]
        for d in range(1, n_ens)
    ]
    for s in range(SUBS):
        for d in range(1, n_ens):
            x_copies[d - 1][s].start()

    for load in loads[:3]:
        load.wait()
    innov_row, obs_row = innov[...], obs[...]

    def weigh(b, _):
        start = pl.multiple_of(b * BLK, BLK)
        column = weight_column(innov_row, obs_row, start)
        value = column * anom[pl.ds(start, BLK), :].astype(F32)
        weighted[pl.ds(pl.multiple_of(start + BLK, BLK), BLK), :] = value.astype(BF16)
        return 0

    lax.fori_loop(0, n_blocks, weigh, 0)

    def localize(b):
        start = pl.multiple_of(b * BLK, BLK)
        ops = jnp.concatenate([local[b, 0], local[b, 1], local[b, 2]], axis=1)
        value = mm(ops, weighted[pl.ds(start, 3 * BLK), :])
        loc_t[:, pl.ds(start, BLK)] = value.T.astype(BF16)

    def inner(b, _):
        localize(b)
        return 0

    loads[3].wait()
    lax.fori_loop(1, n_blocks - 1, inner, 0)

    halo_copy.wait_recv()
    halo_mate = remote(halo.at[parity], halo.at[parity], h_send.at[1], h_recv.at[1], at(tt=mate))
    halo_mate.start()

    def split_map(i, _):
        block = tangent[0, i]
        high = block.astype(BF16)
        low = (block - high.astype(F32)).astype(BF16)
        map_a[i, 0:BLK, :] = high
        map_a[i, BLK : 2 * BLK, :] = low
        turned = block.T
        high = turned.astype(BF16)
        map_f[i, 0:BLK, :] = high
        map_f[i, BLK : 2 * BLK, :] = (turned - high.astype(F32)).astype(BF16)
        return 0

    loads[4].wait()
    loads[5].wait()
    lax.fori_loop(0, n_pieces, split_map, 0)

    for copy in obs_copies:
        copy.wait_recv()
    remote(
        halo.at[1 - parity], halo.at[1 - parity], h_send.at[1], h_recv.at[1], at(tt=mate)
    ).wait_recv()
    for side, first, place in ((0, cells - BLK, 0), (1, 0, cells + BLK)):
        column = weight_column(halo_innov[side], halo_obs[side], first)
        weighted[place : place + BLK, :] = (column * halo[side].astype(F32)).astype(BF16)
    localize(0)
    localize(n_blocks - 1)

    scale = float(cells * n_lon) ** (-0.5)

    def r_copy(d, k, c):
        span = pl.ds(pl.multiple_of(c * chunk, chunk), chunk)
        return remote(
            part_send.at[d - 1, k, span],
            part_recv.at[d - 1, k, span],
            r_send.at[d - 1, k, c],
            r_recv.at[d - 1, k, c],
            at(ll=lax.rem(l + d, n_lon)),
        )

    def partials(k, source):
        for d in range(1, n_lon + 1):
            dest = lax.rem(l + d, n_lon)
            mine = loc_t[pl.ds(pl.multiple_of(dest * rows, rows), rows), :]
            value = (mm(mine, source[...]) * scale).astype(BF16)
            if d < n_lon:
                part_send[d - 1, k] = value
                for c in range(n_chunks):
                    r_copy(d, k, c).start()
            else:
                part_own[k] = value

    partials(0, anom)
    mate_copies = []
    for s in range(SUBS):
        for d in range(1, n_ens):
            x_copies[d - 1][s].wait_recv()
            copy = x_copy(d, s, xf_send, xf_recv, at(tt=mate), other.at[d - 1])
            copy.start()
            mate_copies.append(copy)
    for s in range(SUBS):
        for d in range(1, n_ens):
            span = pl.ds(pl.multiple_of((1 - parity) * half + s * sub, sub), sub)
            remote(
                other.at[d - 1, span],
                other.at[d - 1, span],
                xf_send.at[d - 1, s],
                xf_recv.at[d - 1, s],
                at(tt=mate),
            ).wait_recv()
    for k in range(1, n_ens):
        partials(k, other.at[k - 1])

    slots = [order[0, i] for i in range(n_pieces)]
    inverse = []
    for j in range(n_pieces):
        place = jnp.int32(0)
        for i in range(n_pieces):
            place = jnp.where(slots[i] == j, jnp.int32(i), place)
        inverse.append(place)

    @pl.when(t == 0)
    def _():
        f_in[...] = jnp.zeros_like(f_in)

    @pl.when(t == n_tm - 1)
    def _():
        a_in[...] = jnp.zeros_like(a_in)

    def f_copy(c):
        return remote(f_out.at[c], f_in.at[c], f_send.at[c], f_recv.at[c], at(tt=lax.rem(t + 1, n_tm)))

    def a_copy(c):
        return remote(
            a_out.at[c], a_in.at[c], a_send.at[c], a_recv.at[c], at(tt=lax.rem(t + n_tm - 1, n_tm))
        )

    def gather_force(c):
        span = pl.ds(pl.multiple_of(c * chunk, chunk), chunk)
        for k in range(n_ens):
            total = part_own[k, span, :].astype(F32)
            for d in range(1, n_lon):
                r_copy(d, k, c).wait_recv()
                total = total + part_recv[d - 1, k, span, :].astype(F32)
            base = lax.rem(e - k + n_ens, n_ens) * group
            for q in range(group):
                force[c, base + q] = total[:, q * BLK : (q + 1) * BLK]

    def forward_chunk(c):
        @pl.when(t > 0)
        def _():
            f_copy(c).wait_recv()

        span = pl.ds(pl.multiple_of(c * chunk, chunk), chunk)
        f_now[...] = f_in[c]
        for i in range(n_pieces):
            state = f_now[slots[i]]
            value = mm(jnp.concatenate([state, state], axis=1), map_f[i]) + force[c, i]
            f_out[c, i] = value.astype(BF16)
            fwd_out[0, span, i * BLK : (i + 1) * BLK] = value

        @pl.when(t < n_tm - 1)
        def _():
            f_copy(c).start()

    def apply_force(c):
        for j in range(n_pieces):
            value = force[c, inverse[j]]
            high = value.astype(BF16)
            low = (value - high.astype(F32)).astype(BF16)
            both = map_a[inverse[j]]
            force_a[c, j] = mm(jnp.concatenate([high, high], axis=1), both) + mm(low, both[0:BLK])

    def adjoint_chunk(c):
        @pl.when(t < n_tm - 1)
        def _():
            a_copy(c).wait_recv()

        span = pl.ds(pl.multiple_of(c * chunk, chunk), chunk)
        a_now[...] = a_in[c]
        for j in range(n_pieces):
            state = a_now[inverse[j]]
            value = mm(jnp.concatenate([state, state], axis=1), map_a[inverse[j]]) + force_a[c, j]
            a_out[c, j] = value.astype(BF16)
            adj_out[0, span, j * BLK : (j + 1) * BLK] = value

        @pl.when(t > 0)
        def _():
            a_copy(c).start()

    def turn(s, _):
        @pl.when(s < n_chunks)
        def _():
            gather_force(s)

        c_f = s - LAG * t

        @pl.when((c_f >= 0) & (c_f < n_chunks))
        def _():
            forward_chunk(c_f)

        @pl.when(s < n_chunks)
        def _():
            apply_force(s)

        c_a = s - LAG * (n_tm - 1 - t)

        @pl.when((c_a >= 0) & (c_a < n_chunks))
        def _():
            adjoint_chunk(c_a)

        return 0

    lax.fori_loop(0, LAG * (n_tm - 1) + n_chunks, turn, 0)

    halo_copy.wait_send()
    halo_mate.wait_send()
    for copy in obs_copies + mate_copies:
        copy.wait_send()
    for d in range(1, n_ens):
        for s in range(SUBS):
            x_copies[d - 1][s].wait_send()
    for d in range(1, n_lon):
        for k in range(n_ens):
            for c in range(n_chunks):
                r_copy(d, k, c).wait_send()

    @pl.when(t < n_tm - 1)
    def _():
        for c in range(n_chunks):
            f_copy(c).wait_send()

    @pl.when(t > 0)
    def _():
        for c in range(n_chunks):
            a_copy(c).wait_send()


def store(fwd, adj, fwd_out, adj_out, sem):
    part = fwd.shape[1] // STORES
    copies = []
    for which, (src, dst) in enumerate(((fwd, fwd_out), (adj, adj_out))):
        for i in range(STORES):
            span = pl.ds(i * part, part)
            copies.append(
                pltpu.make_async_copy(src.at[0, span], dst.at[0, span], sem.at[which, i])
            )
    for copy in copies:
        copy.start()
    for copy in copies:
        copy.wait()


def on_device(mesh_dims, anomalies, localization, innovations, obs_cell, tangent_blocks, tangent_order):
    n_tm, n_lon, n_ens = mesh_dims
    cells, cols = anomalies.shape
    rank = cols * n_ens
    rows = cols // n_lon
    chunk = min(32, rows)
    n_chunks = rows // chunk
    pieces = tangent_blocks.shape[1]
    obs = innovations.shape[1]
    vmem = pltpu.VMEM
    dma = pltpu.SemaphoreType.DMA
    state = (n_chunks, pieces, chunk, BLK)
    parts = (max(n_lon - 1, 1), n_ens, rows, cols)
    r_sems = (max(n_lon - 1, 1), n_ens, n_chunks)
    x_sems = (max(n_ens - 1, 1), SUBS)
    in_vmem = pl.BlockSpec(memory_space=pltpu.VMEM)
    out = jax.ShapeDtypeStruct((1, rows, rank), F32)
    states = pl.pallas_call(
        functools.partial(kernel, (n_tm, n_lon, n_ens, rows, chunk)),
        out_shape=(out, out),
        in_specs=[pl.BlockSpec(memory_space=pl.ANY)] * 6,
        out_specs=(in_vmem, in_vmem),
        scratch_shapes=[
            vmem(anomalies.shape, BF16),
            vmem(localization.shape, BF16),
            vmem(innovations.shape, F32),
            vmem(obs_cell.shape, jnp.int32),
            vmem(tangent_blocks.shape, F32),
            pltpu.SMEM(tangent_order.shape, jnp.int32),
            dma((6,)),
            vmem((max(n_ens - 1, 1), cells, cols), BF16),
            vmem((2, BLK, cols), BF16),
            vmem((2, 1, obs), F32),
            vmem((2, 1, obs), jnp.int32),
            vmem((cells + 2 * BLK, cols), BF16),
            vmem((cols, cells), BF16),
            vmem(parts, BF16),
            vmem(parts, BF16),
            vmem((n_ens, rows, cols), BF16),
            vmem(state, F32),
            vmem(state, F32),
            vmem(state, BF16),
            vmem(state, BF16),
            vmem(state, BF16),
            vmem(state, BF16),
            vmem((pieces, chunk, BLK), BF16),
            vmem((pieces, chunk, BLK), BF16),
            vmem((pieces, 2 * BLK, BLK), BF16),
            vmem((pieces, 2 * BLK, BLK), BF16),
            dma(x_sems),
            dma(x_sems),
            dma(x_sems),
            dma(x_sems),
            dma((2,)),
            dma((2,)),
            dma((4,)),
            dma((4,)),
            dma(r_sems),
            dma(r_sems),
            dma((n_chunks,)),
            dma((n_chunks,)),
            dma((n_chunks,)),
            dma((n_chunks,)),
        ],
        compiler_params=pltpu.CompilerParams(
            collective_id=0, has_side_effects=True, vmem_limit_bytes=56 * 1024 * 1024
        ),
    )(anomalies, localization, innovations, obs_cell, tangent_blocks, tangent_order)
    return pl.pallas_call(
        store,
        out_shape=(out, out),
        in_specs=[in_vmem] * 2,
        out_specs=[pl.BlockSpec(memory_space=pl.ANY)] * 2,
        scratch_shapes=[dma((2, STORES))],
        compiler_params=pltpu.CompilerParams(vmem_limit_bytes=56 * 1024 * 1024),
    )(*states)


def solution(mesh):
    placed = (
        P("lon", "ens"),
        P("lon", None, None, None),
        P("tm", "lon"),
        P("tm", "lon"),
        P("tm", None, None, None),
        P("tm", None),
    )
    mesh_dims = tuple(mesh.shape[name] for name in ("tm", "lon", "ens"))
    return jax.shard_map(
        functools.partial(on_device, mesh_dims),
        mesh=mesh,
        in_specs=placed,
        out_specs=(P("tm", ("ens", "lon"), None), P("tm", ("ens", "lon"), None)),
        check_vma=False,
    )
```
